256 devices in a mesh: lat: 64 (over x, z, core), fld: 4 (over y).
Axes of the slice: x: 4, y: 4, z: 8, core: 2. Of those that a mesh axis runs over, the one named last changes fastest.
Arguments:
- grid_fields: float32 [2560, 24, 2688], P('lat', 'fld'), may hold values from -6 to 6
- row_points: int32 [2560], P('lat'), may hold values from 20 to 2688, as said below
- wave_order: int32 [640], replicated, may hold values from 0 to 639, each once
- legendre: bfloat16 [640, 2560, 384], P('lat', 'fld'), may hold values from -6 to 6
- helmholtz_tau: float32 [24], replicated, may hold values from 0.5 to 20
Outputs:
- spectral: float32 [640, 48, 2, 384], P('lat', 'fld')
The draws below stay inside these ranges and needn't reach their ends.
Inputs may be any that keep to these rules, and one draw needn't show every extreme that they name: row_points[r] equals row_points[r + 1280]; the pole rows r = 0 and r = 1280 hold exactly 20 points and the rows r = 1279 and r = 2559 exactly 2688.
All inputs are finite; a program needn't handle non-finite values.
Results may differ from the reference program's by a relative error of at most 0.0029.
Values may be sent and summed in bfloat16 or wider, within the bound.
No kernel may reach another device: no remote copies, remote signals or barrier semaphores. Data moves between devices by JAX's collectives and lax.ppermute only.
A program may use at most 128 MiB of HBM per device.

```python
import math
import jax
import jax.numpy as jnp
from jax import lax

ROWCAP = 2688
NHALF = 384
FLEV = 24
NLAT = 2560
MW = 640


def draw_row_points(key, part):
    key = jax.random.fold_in(key, 11)
    half = NLAT // 2
    index = jnp.arange(half, dtype=jnp.int32)
    base = 20 + (ROWCAP - 20) * index // (half - 1)
    jitter = jax.random.randint(key, (half,), -24, 25, dtype=jnp.int32)
    lengths = jnp.clip(base + jitter, 20, ROWCAP)
    lengths = jnp.where(index == 0, 20, lengths)
    lengths = jnp.where(index == half - 1, ROWCAP, lengths)
    return jnp.concatenate([lengths, lengths]).astype(jnp.int32)


def block_scale(rng, dims, cuts, low, largest):
    def one(axis_at, shards_of):
        heights = jax.random.uniform(jax.random.fold_in(jax.random.fold_in(rng, 6), axis_at), (shards_of,), jnp.float32, low / len(cuts), largest / len(cuts))
        return jnp.repeat(jnp.exp(heights), dims[axis_at] // shards_of).reshape((-1,) + (1,) * (len(dims) - axis_at - 1))

    loudness = one(*cuts[0])
    for cut in cuts[1:]:
        loudness = loudness * one(*cut)
    return loudness


def bell_draw(own_key, shape, scale, bound, shards=(), kind=jnp.bfloat16):
    entries = jax.random.normal(own_key, shape, jnp.float32) * scale
    if len(shards) > 0:
        entries = block_scale(own_key, shape, shards, -0.22, 0.18) * entries
    return jnp.clip(entries, min=-bound, max=bound).astype(kind)


def setup_inputs(seed: int = 0) -> dict:
    keys = jax.random.split(jax.random.key(seed), 6)
    grid_fields = bell_draw(keys[0], (NLAT, FLEV, ROWCAP), 1.0, 6.0, ((0, 64), (1, 4)), jnp.float32)
    row_points = draw_row_points(jax.random.fold_in(keys[5], 71), 0)
    wave_order = jax.random.permutation(keys[2], MW).astype(jnp.int32)
    legendre = bell_draw(keys[3], (MW, NLAT, NHALF), 1.0, 6.0, ((0, 64), (1, 4)))
    helmholtz_tau = jnp.clip(jnp.exp(jax.random.uniform(keys[4], (FLEV,), jnp.float32, math.log(0.5), math.log(20.0))), 0.5, 20.0)
    return {"grid_fields": grid_fields, "row_points": row_points, "wave_order": wave_order, "legendre": legendre, "helmholtz_tau": helmholtz_tau}


def angle_tables(lengths, waves, starts):
    reduced = starts % lengths[:, None]
    product = (waves[None, None, :] * reduced[:, :, None]) % lengths[:, None, None]
    angle = product.astype(jnp.float32) * (2.0 * math.pi) / lengths.astype(jnp.float32)[:, None, None]
    return jnp.cos(angle), jnp.sin(angle)


def row_transform(rows, lengths, waves):
    group, levels, points = rows.shape
    block_len = 128
    blocks = points // block_len
    offsets = jnp.broadcast_to(jnp.arange(block_len, dtype=jnp.int32), (group, block_len))
    cos_in, sin_in = angle_tables(lengths, waves, offsets)
    table = jnp.concatenate([cos_in, sin_in], axis=2)
    starts = jnp.broadcast_to(jnp.arange(blocks, dtype=jnp.int32) * block_len, (group, blocks))
    cos_out, sin_out = angle_tables(lengths, waves, starts)
    width = waves.shape[0]
    pieces = rows.reshape((group, levels, blocks, block_len))
    partial_sums = jnp.einsum('rlbj,rjm->rblm', pieces, table, precision=lax.Precision.HIGHEST)
    cos_part = partial_sums[..., :width]
    sin_part = partial_sums[..., width:]
    real_part = jnp.sum(cos_part * cos_out[:, :, None, :] - sin_part * sin_out[:, :, None, :], axis=1)
    imag_part = -jnp.sum(sin_part * cos_out[:, :, None, :] + cos_part * sin_out[:, :, None, :], axis=1)
    scale = jnp.where(2 * waves[None, :] < lengths[:, None], 1.0 / lengths.astype(jnp.float32)[:, None], jnp.zeros((), jnp.float32))
    return jnp.stack([real_part, imag_part], axis=2) * scale[:, None, None, :]


def reference(grid_fields, row_points, wave_order, legendre, helmholtz_tau):
    count = grid_fields.shape[0]
    half = count // 2
    inside = jnp.arange(ROWCAP, dtype=jnp.int32)[None, :] < row_points[:, None]
    masked = jnp.where(inside[:, None, :], grid_fields, jnp.zeros((), jnp.float32))
    group = math.gcd(count, 8)
    grouped = masked.reshape((count // group, group, FLEV, ROWCAP))
    lengths = row_points.reshape((count // group, group))

    def one_group(pair):
        return row_transform(pair[0], pair[1], wave_order)

    spectra = lax.map(one_group, (grouped, lengths)).reshape((count, FLEV, 2, MW))
    north = spectra[:half]
    south = spectra[half:]
    folded = jnp.concatenate([north + south, north - south], axis=0)
    folded_low = folded.astype(jnp.bfloat16)
    by_wave = jnp.transpose(folded_low, (3, 0, 1, 2))

    def project(pair):
        values, table = pair
        values = values.astype(jnp.float32)
        table = table.astype(jnp.float32)
        even = jnp.einsum('rlc,rq->lcq', values[:half], table[:half], precision=lax.Precision.HIGHEST)
        odd = jnp.einsum('rlc,rq->lcq', values[half:], table[half:], precision=lax.Precision.HIGHEST)
        return jnp.stack([even, odd])

    projected = lax.map(project, (by_wave, legendre))
    degree = wave_order[:, None, None] + 2 * jnp.arange(NHALF, dtype=jnp.int32)[None, None, :] + jnp.arange(2, dtype=jnp.int32)[None, :, None]
    degree = degree.astype(jnp.float32)
    shape_term = degree * (degree + 1.0) / float((2 * NHALF) ** 2)
    operator = 1.0 + helmholtz_tau[None, None, :, None, None] * shape_term[:, :, None, None, :]
    return (projected / operator).reshape((MW, 2 * FLEV, 2, NHALF))
```

```python
import functools

import jax
import jax.numpy as jnp
from jax import lax
from jax.experimental import pallas as pl
from jax.experimental.pallas import tpu as pltpu
from jax.sharding import PartitionSpec as P

SIN = (6.283184916495431, -41.341589232688555, 81.59994332978103, -76.61447253122742, 41.34288235446962, -12.471243534881289)
COS = (0.9999999890590217, -19.73920449945379, 64.93911745989134, -85.45013953081433, 60.16763095040022, -25.96759924640718, 6.528658158395448)
MAGIC = 12582912.0


def horner(coefs, x):
    acc = jnp.full_like(x, coefs[-1])
    for c in coefs[-2::-1]:
        acc = acc * x + c
    return acc


def unit(product, length, inverse):
    turns = (product * inverse + MAGIC) - MAGIC
    u = (product - turns * length) * inverse
    v = u * u
    return horner(COS, v), horner(SIN, v) * u


def dft_kernel(groups, base, points, levels, slots, len_ref, wave_ref, x_ref, o_ref, xs, a, o):
    g = pl.program_id(0)
    blocks = points // 128
    owners = wave_ref.shape[1] // slots
    rows = 8 * groups
    tiles = wave_ref.shape[1] // 128
    height = blocks * 8

    @pl.when(g == 0)
    def _():
        xs[...] = jnp.zeros_like(xs)
        a[...] = jnp.zeros_like(a)

    for b in range(blocks):
        for l in range(levels):
            xs[pl.ds(b * 64 + l * 8, 8), :] = x_ref[l, :, b * 128 : (b + 1) * 128]

    lane = lax.broadcasted_iota(jnp.int32, (8, 128), 1)
    sub = lax.broadcasted_iota(jnp.int32, (8, 128), 0).astype(jnp.float32)
    low = lane < 64

    def one_row(r):
        length = len_ref[base * 8 + g * 8 + r]
        full = jnp.zeros((8, 128), jnp.int32) + length
        lf = full.astype(jnp.float32)
        inv = 1.0 / lf
        x = xs[pl.ds(r, height, stride=8), :].reshape(blocks, 8, 128)
        x = jnp.concatenate([jnp.where(lane + 128 * b < full, x[b], 0.0) for b in range(blocks)], axis=0)
        hi = x.astype(jnp.bfloat16)
        lo = (x - hi.astype(jnp.float32)).astype(jnp.bfloat16)
        lhs = jnp.concatenate([hi, lo, hi], axis=1)
        out = []
        for t in range(tiles):
            wave = wave_ref[:, t * 128 : (t + 1) * 128] + jnp.zeros((8, 128), jnp.float32)
            c, s = unit(wave * sub, lf, inv)
            c8, s8 = unit(wave * 8.0, lf, inv)
            cw, sw = unit(wave * 128.0, lf, inv)
            cs, ss = [c], [s]
            for _ in range(15):
                c, s = c * c8 - s * s8, s * c8 + c * s8
                cs.append(c)
                ss.append(s)
            table = jnp.concatenate([jnp.concatenate(cs, axis=0), jnp.concatenate(ss, axis=0)], axis=1)
            thi = table.astype(jnp.bfloat16)
            tlo = (table - thi.astype(jnp.float32)).astype(jnp.bfloat16)
            rhs = jnp.concatenate([thi, thi, tlo], axis=0)
            part = jnp.dot(lhs, rhs, preferred_element_type=jnp.float32)
            part = part.reshape(blocks, 8, 256)
            re = part[blocks - 1, :, :128]
            im = part[blocks - 1, :, 128:]
            for b in range(blocks - 2, -1, -1):
                re, im = (re * cw - im * sw) + part[b, :, :128], (im * cw + re * sw) + part[b, :, 128:]
            scale = jnp.where(2.0 * wave < lf, inv, 0.0)
            out.append((re * scale, -(im * scale)))
        return out

    def pair(p, _):
        r0 = p * 2
        first = one_row(r0)
        second = one_row(r0 + 1)
        for t in range(tiles):
            for c in range(2):
                u, v = first[t][c], second[t][c]
                even = jnp.where(low, u, pltpu.roll(v, 64, 1))
                odd = jnp.where(low, pltpu.roll(u, 64, 1), v)
                a[pl.ds(c * slots + 2 * t, levels, stride=2 * slots), :] = even[:levels]
                a[pl.ds(c * slots + 2 * t + 1, levels, stride=2 * slots), :] = odd[:levels]
        turned = a[...].T
        o[pl.ds(g * 8 + r0, owners, stride=rows), :] = turned[:owners]
        o[pl.ds(g * 8 + r0 + 1, owners, stride=rows), :] = turned[owners:]
        return 0

    lax.fori_loop(0, 4, pair, 0)

    @pl.when(g == groups - 1)
    def _():
        o_ref[...] = o[...].astype(jnp.bfloat16)


def transform(x, lengths, waves, slots, base, groups):
    levels, count, points = x.shape
    owners = waves.shape[1] // slots
    rows = 8 * groups
    kernel = functools.partial(dft_kernel, groups, base, points, levels, slots)
    flops = 2 * 6 * rows * levels * points * waves.shape[1]
    return pl.pallas_call(
        kernel,
        grid=(groups,),
        out_shape=jax.ShapeDtypeStruct((owners * rows, 128), jnp.bfloat16),
        in_specs=[
            pl.BlockSpec(memory_space=pltpu.SMEM),
            pl.BlockSpec((1, waves.shape[1]), lambda g: (0, 0)),
            pl.BlockSpec((levels, 8, points), lambda g: (0, g + base, 0)),
        ],
        out_specs=pl.BlockSpec((owners * rows, 128), lambda g: (0, 0)),
        scratch_shapes=[
            pltpu.VMEM((points // 128 * 64, 128), jnp.float32),
            pltpu.VMEM((128, 128), jnp.float32),
            pltpu.VMEM((owners * rows, 128), jnp.float32),
        ],
        compiler_params=pltpu.CompilerParams(vmem_limit_bytes=24 * 1024 * 1024),
        cost_estimate=pl.CostEstimate(flops=flops, bytes_accessed=rows * levels * points * 4, transcendentals=0),
    )(lengths, waves, x)


def legendre_kernel(chunks, count, halves, levels, slots, sign_ref, half_ref, *refs):
    parts = refs[: len(chunks)]
    leg_ref, kept_ref, given_ref, x, xt = refs[len(chunks) :]
    fields = parts[0].shape[0]
    total = x.shape[0]
    sources = total // count
    width = 2 * levels * slots
    sign = sign_ref[0]
    for f in range(fields):
        for (base, groups), part in zip(chunks, parts):
            rows = 8 * groups
            north = part[f, 0].astype(jnp.float32)
            south = part[f, 1].astype(jnp.float32)
            both = north + sign * south
            for i in range(sources):
                x[pl.ds(i * count + base * 8, rows), :] = both[i * rows : (i + 1) * rows]
        for k in range(0, total, 128):
            xt[k // 128, pl.ds(f * width, width), :] = x[pl.ds(k, 128), :].T[:width]
    here = half_ref[0] == 0
    tall = fields * 2 * levels

    def one_slot(s, _):
        lhs = jnp.concatenate([xt[k, pl.ds(s, tall, stride=slots), :] for k in range(total // 128)], axis=1)
        hi = lhs.astype(jnp.bfloat16)
        lo = (lhs - hi.astype(jnp.float32)).astype(jnp.bfloat16)
        both = jnp.concatenate([hi, lo], axis=0)
        res = jnp.dot(both, leg_ref[s], preferred_element_type=jnp.float32)
        res = res[:tall] + res[tall:]
        upper, lower = res[: tall // 2], res[tall // 2 :]
        kept_ref[s] = jnp.where(here, upper, lower)
        given_ref[s] = jnp.where(here, lower, upper)
        return 0

    lax.fori_loop(0, slots, one_slot, 0)


def project(parts, legendre, sign, half, chunks, count, levels):
    slots, total, coeffs = legendre.shape
    fields = parts[0].shape[0]
    width = 2 * levels * slots
    tall = fields * 2 * levels
    shape = jax.ShapeDtypeStruct((slots, tall // 2, coeffs), jnp.float32)
    kernel = functools.partial(legendre_kernel, chunks, count, 2, levels, slots)
    vmem = pl.BlockSpec(memory_space=pltpu.VMEM)
    smem = pl.BlockSpec(memory_space=pltpu.SMEM)
    return pl.pallas_call(
        kernel,
        out_shape=(shape, shape),
        in_specs=[smem, smem] + [vmem] * (len(parts) + 1),
        out_specs=(vmem, vmem),
        scratch_shapes=[
            pltpu.VMEM((total, 128), jnp.float32),
            pltpu.VMEM((total // 128, fields * width, 128), jnp.float32),
        ],
        compiler_params=pltpu.CompilerParams(vmem_limit_bytes=24 * 1024 * 1024),
        cost_estimate=pl.CostEstimate(flops=4 * slots * tall * total * coeffs, bytes_accessed=slots * total * coeffs * 2, transcendentals=0),
    )(sign, half, *parts, legendre)


CHUNKS = ((0, 5),)


def body(grid_fields, row_points, wave_order, legendre, helmholtz_tau):
    lat_count = lax.axis_size("lat")
    fld_count = lax.axis_size("fld")
    lat_index = lax.axis_index("lat")
    fld_index = lax.axis_index("fld")
    count, levels, _ = grid_fields.shape
    slots, total, coeffs = legendre.shape
    x = jnp.transpose(grid_fields, (1, 0, 2))
    waves = jnp.transpose(wave_order.reshape((lat_count, slots))).reshape((1, lat_count * slots))
    waves = waves.astype(jnp.float32)
    near = total // count
    parts = []
    for base, groups in CHUNKS:
        rows = 8 * groups
        outgoing = transform(x, row_points, waves, slots, base, groups)
        arrived = lax.all_to_all(outgoing, "lat", split_axis=0, concat_axis=0, tiled=True)
        arrived = arrived.reshape((2, 2, near * rows, 128)).transpose((1, 0, 2, 3))
        sent = jnp.concatenate([arrived, arrived], axis=0)
        got = lax.all_to_all(sent, "fld", split_axis=0, concat_axis=0, tiled=True)
        parts.append(got)
    parity = fld_index // 2
    half = fld_index % 2
    sign = (1 - 2 * parity).astype(jnp.float32).reshape((1,))
    kept, given = project(parts, legendre, sign, half.astype(jnp.int32).reshape((1,)), CHUNKS, count, levels)
    route = [(i, i ^ 1) for i in range(fld_count)]
    combined = kept + lax.ppermute(given, "fld", route)
    half_levels = levels * fld_count // 2
    owned = lax.dynamic_slice_in_dim(wave_order, lat_index * slots, slots)
    degree = owned[:, None] + 2 * jnp.arange(coeffs, dtype=jnp.int32)[None, :] + parity
    degree = degree.astype(jnp.float32)
    shape_term = degree * (degree + 1.0) / float((2 * coeffs) ** 2)
    rates = lax.dynamic_slice_in_dim(helmholtz_tau, half * half_levels, half_levels)
    operator = 1.0 + rates[None, :, None, None] * shape_term[:, None, None, :]
    return combined.reshape((slots, half_levels, 2, coeffs)) / operator


def solution(mesh):
    in_specs = (P("lat", "fld", None), P("lat"), P(), P("lat", "fld", None), P())
    out_specs = P("lat", "fld", None, None)
    return jax.shard_map(body, mesh=mesh, in_specs=in_specs, out_specs=out_specs, check_vma=False)
```

```python
import functools

import jax
import jax.numpy as jnp
from jax import lax
from jax.experimental import pallas as pl
from jax.experimental.pallas import tpu as pltpu
from jax.sharding import PartitionSpec as P

SIN = (6.283184916495431, -41.341589232688555, 81.59994332978103, -76.61447253122742, 41.34288235446962, -12.471243534881289)
COS = (0.9999999890590217, -19.73920449945379, 64.93911745989134, -85.45013953081433, 60.16763095040022, -25.96759924640718, 6.528658158395448)
MAGIC = 12582912.0
MIB = 1024 * 1024


def horner(coefs, x):
    acc = jnp.full_like(x, coefs[-1])
    for c in coefs[-2::-1]:
        acc = acc * x + c
    return acc


def unit(product, length, inverse):
    turns = (product * inverse + MAGIC) - MAGIC
    u = (product - turns * length) * inverse
    v = u * u
    return horner(COS, v), horner(SIN, v) * u


def times(p, q):
    return p[0] * q[0] - p[1] * q[1], p[1] * q[0] + p[0] * q[1]


def pick(v, t):
    return jnp.broadcast_to(v[t : t + 1], (8, 128))


def dft_kernel(groups, base, levels, slots, len_ref, south_ref, wave_ref, x_hbm, give_ref, keep_ref, xe, xo, fold, wv, wj, a, o, x_buf, x_sem):
    g = pl.program_id(0)
    blocks = x_hbm.shape[2] // 128
    slot = lax.rem(g, 2)

    def fetch(i, place):
        at = pl.ds(pl.multiple_of((base + i) * 8, 8), 8)
        return pltpu.make_async_copy(x_hbm.at[:, at, :], x_buf.at[place], x_sem.at[place])

    tiles = slots // 2
    rows = 8 * groups
    height = blocks * 8
    lane = lax.broadcasted_iota(jnp.int32, (8, 128), 1)
    sub = lax.broadcasted_iota(jnp.int32, (8, 128), 0)
    low = lane < 64

    @pl.when(g == 0)
    def _():
        fetch(0, 0).start()
        xe[...] = jnp.zeros_like(xe)
        xo[...] = jnp.zeros_like(xo)
        a[...] = jnp.zeros_like(a)
        point = lax.broadcasted_iota(jnp.int32, (256, 256), 0) % 128
        column = lax.broadcasted_iota(jnp.int32, (256, 256), 1)
        k = column % 64
        plus = jnp.where(point == 64 + k, 1.0, 0.0)
        minus = jnp.where(point == 63 - k, 1.0, 0.0)
        fold[...] = jnp.where(column < 128, plus + minus, plus - minus).astype(jnp.bfloat16)
        order = wave_ref[...]
        order = jnp.concatenate([order >> 5, order & 31], axis=0).astype(jnp.float32).astype(jnp.bfloat16)
        source = lax.broadcasted_iota(jnp.int32, (128, 128), 0)
        target = lax.broadcasted_iota(jnp.int32, (128, 128), 1)
        wv[...] = jnp.zeros_like(wv)
        for t in range(tiles):
            index = (target % 64) * slots + 2 * t + target // 64
            chosen = jnp.where(index % 128 == source, 1.0, 0.0).astype(jnp.bfloat16)
            found = jnp.dot(order, chosen, preferred_element_type=jnp.float32)
            found = found[:tiles] * 32.0 + found[tiles:]
            here = index[:tiles] // 128 == source[:tiles]
            wv[t : t + 1, :] = jnp.sum(jnp.where(here, found, 0.0), axis=0, keepdims=True)
        wide = wv[...]
        for i, j in enumerate((16.0, 256.0, 127.0)):
            wj[8 * i : 8 * i + 8, :] = wide * j

    fetch(g, slot).wait()

    @pl.when(g + 1 < groups)
    def _():
        fetch(g + 1, 1 - slot).start()

    x_ref = x_buf.at[slot]
    lengths = jnp.zeros((8, 128), jnp.int32)
    for i in range(8):
        lengths = jnp.where(sub == i, len_ref[(base + g) * 8 + i], lengths)
    for l in range(levels):
        x = [jnp.where(lane + 128 * b < lengths, x_ref[l, :, b * 128 : (b + 1) * 128], 0.0) for b in range(blocks)]
        x = jnp.concatenate(x, axis=0)
        hi = x.astype(jnp.bfloat16)
        lo = (x - hi.astype(jnp.float32)).astype(jnp.bfloat16)
        both = jnp.dot(jnp.concatenate([hi, lo], axis=1), fold[...], preferred_element_type=jnp.float32)
        for ref, v in ((xe, both[:, :128]), (xo, both[:, 128:])):
            top = v.astype(jnp.bfloat16).astype(jnp.float32)
            v = jnp.where(lax.broadcasted_iota(jnp.int32, v.shape, 1) < 64, top, v - top)
            for b in range(blocks):
                ref[pl.ds(b * 64 + l * 8, 8), :] = v[b * 8 : b * 8 + 8]

    def one_row(r):
        length = len_ref[(base + g) * 8 + r]
        lf = (jnp.zeros((8, 128), jnp.int32) + length).astype(jnp.float32)
        inv = 1.0 / lf
        two = lf * 2.0
        half = inv * 0.5
        scale = jnp.where(2.0 * wv[...] < lf, inv, 0.0)
        c8, s8 = unit(wj[0:8, :], two, half)
        cw, sw = unit(wj[8:16, :], two, half)
        cz, sz = unit(wj[16:24, :], two, half)
        cz, sz = cz * scale, sz * scale
        le = xe[pl.ds(r, height, stride=8), :].astype(jnp.bfloat16)
        lo = xo[pl.ds(r, height, stride=8), :].astype(jnp.bfloat16)
        le = jnp.concatenate([le, le], axis=1)
        lo = jnp.concatenate([lo, lo], axis=1)
        odd = (2 * sub + 1).astype(jnp.float32)

        def tables(t):
            c, s = unit(pick(wv[...], t) * odd, two, half)
            cs, ss = [c], [s]
            step = (pick(c8, t), pick(s8, t))
            for level in range(3):
                more = [times(e, step) for e in zip(cs, ss)]
                cs += [m[0] for m in more]
                ss += [m[1] for m in more]
                if level < 2:
                    step = times(step, step)
            pair = []
            for v in (cs, ss):
                v = jnp.concatenate(v, axis=0)
                top = v.astype(jnp.bfloat16)
                rest = (v - top.astype(jnp.float32)).astype(jnp.bfloat16)
                pair.append(jnp.concatenate([top, top, rest, rest], axis=0))
            return pair

        out = []
        for t in range(0, tiles, 2):
            group = [tables(u) for u in range(t, min(t + 2, tiles))]
            cos = jnp.concatenate([e[0] for e in group], axis=1)
            sin = jnp.concatenate([e[1] for e in group], axis=1)
            even = jnp.dot(le, cos, preferred_element_type=jnp.float32).reshape(blocks, 8, cos.shape[1])
            odds = jnp.dot(lo, sin, preferred_element_type=jnp.float32).reshape(blocks, 8, cos.shape[1])
            for i in range(len(group)):
                at = slice(128 * i, 128 * i + 128)
                turn = (pick(cw, t + i), pick(sw, t + i))
                total = (even[blocks - 1, :, at], odds[blocks - 1, :, at])
                for b in range(blocks - 2, -1, -1):
                    total = times(total, turn)
                    total = (total[0] + even[b, :, at], total[1] + odds[b, :, at])
                re, im = times(total, (pick(cz, t + i), pick(sz, t + i)))
                out.append((re, -im))
        return out

    def pair(p, _):
        r0 = p * 2
        first = one_row(r0)
        second = one_row(r0 + 1)
        for t in range(tiles):
            for c in range(2):
                u, v = first[t][c], second[t][c]
                even = jnp.where(low, u, pltpu.roll(v, 64, 1))
                odd = jnp.where(low, pltpu.roll(u, 64, 1), v)
                a[p, pl.ds(c * slots + 2 * t, levels, stride=2 * slots), :] = even[:levels]
                a[p, pl.ds(c * slots + 2 * t + 1, levels, stride=2 * slots), :] = odd[:levels]
        turned = a[p].T
        o[pl.ds(g * 8 + r0, 64, stride=rows), :] = turned[:64]
        o[pl.ds(g * 8 + r0 + 1, 64, stride=rows), :] = turned[64:]
        return 0

    for p in range(4):
        pair(p, 0)

    @pl.when(g == groups - 1)
    def _():
        mine = south_ref[0] * (32 * rows)
        keep_ref[...] = o[pl.ds(pl.multiple_of(mine, 32 * rows), 32 * rows), :]
        give_ref[...] = o[pl.ds(pl.multiple_of(32 * rows - mine, 32 * rows), 32 * rows), :].astype(jnp.bfloat16)


def transform(x, lengths, south, waves, slots, base, groups):
    levels, count, points = x.shape
    rows = 8 * groups
    kernel = functools.partial(dft_kernel, groups, base, levels, slots)
    flops = 2 * 6 * rows * levels * points * 640
    whole = pl.BlockSpec((32 * rows, 128), lambda g: (0, 0))
    return pl.pallas_call(
        kernel,
        grid=(groups,),
        out_shape=(
            jax.ShapeDtypeStruct((32 * rows, 128), jnp.bfloat16),
            jax.ShapeDtypeStruct((32 * rows, 128), jnp.float32),
        ),
        in_specs=[
            pl.BlockSpec(memory_space=pltpu.SMEM),
            pl.BlockSpec(memory_space=pltpu.SMEM),
            pl.BlockSpec((slots // 2, 128), lambda g: (0, 0)),
            pl.BlockSpec(memory_space=pltpu.HBM),
        ],
        out_specs=(whole, whole),
        scratch_shapes=[
            pltpu.VMEM((points // 128 * 64, 128), jnp.float32),
            pltpu.VMEM((points // 128 * 64, 128), jnp.float32),
            pltpu.VMEM((256, 256), jnp.bfloat16),
            pltpu.VMEM((8, 128), jnp.float32),
            pltpu.VMEM((24, 128), jnp.float32),
            pltpu.VMEM((4, 128, 128), jnp.float32),
            pltpu.VMEM((64 * rows, 128), jnp.float32),
            pltpu.VMEM((2, levels, 8, points), jnp.float32),
            pltpu.SemaphoreType.DMA((2,)),
        ],
        compiler_params=pltpu.CompilerParams(vmem_limit_bytes=LIMITS[base > 0] * MIB),
        cost_estimate=pl.CostEstimate(flops=flops, bytes_accessed=rows * levels * points * 4, transcendentals=0),
    )(lengths, south, waves, x)


def fold_kernel(chunks, south_ref, *refs):
    n = len(chunks)
    o_ref = refs[-1]
    sign = 1.0 - 2.0 * south_ref[0].astype(jnp.float32)

    def two_owners(j, _):
        parts = [[], [], [], []]
        for i, (_, groups) in enumerate(chunks):
            rows = 16 * groups
            at = pl.ds(pl.multiple_of(j * rows, rows), rows)
            other = refs[i][at, :].astype(jnp.float32)
            mine = refs[n + i][at, :]
            plus = mine + other
            minus = (mine - other) * sign
            for k in range(2):
                parts[2 * k].append(plus[k * rows // 2 : (k + 1) * rows // 2])
                parts[2 * k + 1].append(minus[k * rows // 2 : (k + 1) * rows // 2])
        block = jnp.concatenate([e for part in parts for e in part], axis=0)
        size = block.shape[0]
        o_ref[pl.ds(pl.multiple_of(j * size, size), size), :] = block.astype(jnp.bfloat16)
        return 0

    lax.fori_loop(0, 16, two_owners, 0, unroll=2)


def folded(others, mine, south, chunks):
    total = sum(8 * groups for _, groups in chunks)
    vmem = pl.BlockSpec(memory_space=pltpu.VMEM)
    return pl.pallas_call(
        functools.partial(fold_kernel, chunks),
        out_shape=jax.ShapeDtypeStruct((64 * total, 128), jnp.bfloat16),
        in_specs=[pl.BlockSpec(memory_space=pltpu.SMEM)] + [vmem] * (2 * len(chunks)),
        out_specs=vmem,
        compiler_params=pltpu.CompilerParams(vmem_limit_bytes=16 * MIB),
        cost_estimate=pl.CostEstimate(flops=64 * total * 256, bytes_accessed=0, transcendentals=0),
    )(south, *others, *mine)


def load_kernel(hbm, after, vmem, sem):
    copy = pltpu.make_async_copy(hbm, vmem, sem)
    copy.start()
    copy.wait()


def load(array, after):
    return pl.pallas_call(
        load_kernel,
        out_shape=jax.ShapeDtypeStruct(array.shape, array.dtype),
        in_specs=[pl.BlockSpec(memory_space=pltpu.HBM), pl.BlockSpec(memory_space=pl.ANY)],
        out_specs=pl.BlockSpec(memory_space=pltpu.VMEM),
        scratch_shapes=[pltpu.SemaphoreType.DMA],
        compiler_params=pltpu.CompilerParams(vmem_limit_bytes=16 * MIB),
        cost_estimate=pl.CostEstimate(flops=0, bytes_accessed=array.size * 2, transcendentals=0),
    )(array, after)


def legendre_kernel(levels, slots, half_ref, place_ref, *refs):
    fields = len(refs) - 4
    parts = refs[:fields]
    leg_ref, kept_ref, given_ref, xt = refs[fields:]
    total = parts[0].shape[0]
    width = 2 * levels * slots
    for i, part in enumerate(parts):
        at = pl.multiple_of(place_ref[i] * width, 8)
        for k in range(0, total, 128):
            xt[k // 128, pl.ds(at, width), :] = part[pl.ds(k, 128), :].astype(jnp.float32).T[:width]
    here = half_ref[0] == 0
    tall = fields * 2 * levels

    def one_slot(s, _):
        lhs = jnp.concatenate([xt[k, pl.ds(s, tall, stride=slots), :] for k in range(total // 128)], axis=1)
        res = jnp.dot(lhs.astype(jnp.bfloat16), leg_ref[s], preferred_element_type=jnp.float32)
        upper, lower = res[: tall // 2], res[tall // 2 :]
        kept_ref[s] = jnp.where(here, upper, lower)
        given_ref[s] = jnp.where(here, lower, upper).astype(given_ref.dtype)
        return 0

    lax.fori_loop(0, slots, one_slot, 0, unroll=2)


def project(parts, legendre, half, places, levels, slots):
    _, total, coeffs = legendre.shape
    fields = len(parts)
    width = 2 * levels * slots
    tall = fields * 2 * levels
    vmem = pl.BlockSpec(memory_space=pltpu.VMEM)
    smem = pl.BlockSpec(memory_space=pltpu.SMEM)
    return pl.pallas_call(
        functools.partial(legendre_kernel, levels, slots),
        out_shape=(
            jax.ShapeDtypeStruct((slots, tall // 2, coeffs), jnp.float32),
            jax.ShapeDtypeStruct((slots, tall // 2, coeffs), PARTIAL),
        ),
        in_specs=[smem, smem] + [vmem] * (fields + 1),
        out_specs=(vmem, vmem),
        scratch_shapes=[pltpu.VMEM((total // 128, fields * width, 128), jnp.float32)],
        compiler_params=pltpu.CompilerParams(vmem_limit_bytes=24 * MIB),
        cost_estimate=pl.CostEstimate(flops=4 * slots * tall * total * coeffs, bytes_accessed=slots * total * coeffs * 2, transcendentals=0),
    )(half, places, *parts, legendre)


CHUNKS = ((0, 3), (3, 2))
PARTIAL = jnp.bfloat16
LIMITS = (60, 20)


def body(grid_fields, row_points, wave_order, legendre, helmholtz_tau):
    lat_count = lax.axis_size("lat")
    fld_count = lax.axis_size("fld")
    lat_index = lax.axis_index("lat")
    fld_index = lax.axis_index("fld")
    count, levels, _ = grid_fields.shape
    slots, total, coeffs = legendre.shape
    owners = lat_count // 2
    x = jnp.transpose(grid_fields, (1, 0, 2))
    waves = wave_order.reshape((slots // 2, 128))
    south = (lat_index // owners).astype(jnp.int32).reshape((1,))
    across = [(i, i ^ owners) for i in range(lat_count)]
    sides = [list(range(owners)), list(range(owners, 2 * owners))]
    others, mine = [], []
    for base, groups in CHUNKS:
        give, keep = transform(x, row_points, south, waves, slots, base, groups)
        others.append(lax.ppermute(give, "lat", across))
        mine.append(keep)
    outgoing = folded(others, mine, south, CHUNKS)
    arrived = lax.all_to_all(outgoing, "lat", split_axis=0, concat_axis=0, tiled=True, axis_index_groups=sides)
    legendre = load(legendre, outgoing)
    arrived = arrived.reshape((2, owners // 2, 2, count, 128)).transpose((2, 0, 1, 3, 4)).reshape((fld_count, total, 128))
    parts, places = [], []
    for k in range(fld_count):
        block = lax.dynamic_index_in_dim(arrived, fld_index ^ k, 0, keepdims=False)
        if k:
            block = lax.ppermute(block, "fld", [(i, i ^ k) for i in range(fld_count)])
        parts.append(block)
        places.append(fld_index ^ k)
    places = jnp.stack(places).astype(jnp.int32)
    parity = fld_index // 2
    half = fld_index % 2
    kept, given = project(parts, legendre, half.astype(jnp.int32).reshape((1,)), places, levels, slots)
    combined = kept + lax.ppermute(given, "fld", [(i, i ^ 1) for i in range(fld_count)]).astype(jnp.float32)
    half_levels = levels * fld_count // 2
    owned = lax.dynamic_slice_in_dim(wave_order, lat_index * slots, slots)
    degree = owned[:, None] + 2 * jnp.arange(coeffs, dtype=jnp.int32)[None, :] + parity
    degree = degree.astype(jnp.float32)
    shape_term = degree * (degree + 1.0) / float((2 * coeffs) ** 2)
    rates = lax.dynamic_slice_in_dim(helmholtz_tau, half * half_levels, half_levels)
    operator = 1.0 + rates[None, :, None, None] * shape_term[:, None, None, :]
    return combined.reshape((slots, half_levels, 2, coeffs)) / operator


def solution(mesh):
    in_specs = (P("lat", "fld", None), P("lat"), P(), P("lat", "fld", None), P())
    out_specs = P("lat", "fld", None, None)
    return jax.shard_map(body, mesh=mesh, in_specs=in_specs, out_specs=out_specs, check_vma=False)
```

```python
import functools

import jax
import jax.numpy as jnp
from jax import lax
from jax.experimental import pallas as pl
from jax.experimental.pallas import tpu as pltpu
from jax.sharding import PartitionSpec as P

SIN = (6.283184916495431, -41.341589232688555, 81.59994332978103, -76.61447253122742, 41.34288235446962, -12.471243534881289)
COS = (0.9999999890590217, -19.73920449945379, 64.93911745989134, -85.45013953081433, 60.16763095040022, -25.96759924640718, 6.528658158395448)
MAGIC = 12582912.0
MIB = 1024 * 1024


def horner(coefs, x):
    acc = jnp.full_like(x, coefs[-1])
    for c in coefs[-2::-1]:
        acc = acc * x + c
    return acc


def unit(product, length, inverse):
    turns = (product * inverse + MAGIC) - MAGIC
    u = (product - turns * length) * inverse
    v = u * u
    return horner(COS, v), horner(SIN, v) * u


def times(p, q):
    return p[0] * q[0] - p[1] * q[1], p[1] * q[0] + p[0] * q[1]


def pick(v, t):
    return jnp.broadcast_to(v[t : t + 1], (8, 128))


def dft_kernel(groups, base, levels, slots, len_ref, south_ref, wave_ref, x_hbm, give_ref, keep_ref, xe, xo, fold, wv, wj, a, o, x_buf, x_sem):
    g = pl.program_id(0)
    blocks = x_hbm.shape[2] // 128
    slot = lax.rem(g, 2)

    def eighth(t):
        return (tiles + t, 0) if tiles + t < 8 else (2 * tiles + t, 1)

    def fetch(i, place):
        at = pl.ds(pl.multiple_of((base + i) * 8, 8), 8)
        return pltpu.make_async_copy(x_hbm.at[:, at, :], x_buf.at[place], x_sem.at[place])

    tiles = slots // 2
    rows = 8 * groups
    height = blocks * 8
    middle = blocks // 2
    lane = lax.broadcasted_iota(jnp.int32, (8, 128), 1)
    sub = lax.broadcasted_iota(jnp.int32, (8, 128), 0)
    low = lane < 64

    @pl.when(g == 0)
    def _():
        fetch(0, 0).start()
        xe[...] = jnp.zeros_like(xe)
        xo[...] = jnp.zeros_like(xo)
        a[...] = jnp.zeros_like(a)
        point = lax.broadcasted_iota(jnp.int32, (256, 256), 0) & 127
        column = lax.broadcasted_iota(jnp.int32, (256, 256), 1)
        k = column & 63
        plus = jnp.where(point == 64 + k, 1.0, 0.0)
        minus = jnp.where(point == 63 - k, 1.0, 0.0)
        fold[...] = jnp.where(column < 128, plus + minus, plus - minus).astype(jnp.bfloat16)
        order = wave_ref[...]
        order = jnp.concatenate([order >> 5, order & 31], axis=0).astype(jnp.float32).astype(jnp.bfloat16)
        source = lax.broadcasted_iota(jnp.int32, (128, 128), 0)
        target = lax.broadcasted_iota(jnp.int32, (128, 128), 1)
        wv[...] = jnp.zeros_like(wv)
        for t in range(tiles):
            index = (target & 63) * slots + 2 * t + (target >> 6)
            chosen = jnp.where((index & 127) == source, 1.0, 0.0).astype(jnp.bfloat16)
            found = jnp.dot(order, chosen, preferred_element_type=jnp.float32)
            found = found[:tiles] * 32.0 + found[tiles:]
            here = (index[:tiles] >> 7) == source[:tiles]
            wv[t : t + 1, :] = jnp.sum(jnp.where(here, found, 0.0), axis=0, keepdims=True)
        wide = wv[...]
        wj[0:8, :] = wide * 256.0
        wj[8:16, :] = wide * (256.0 * middle + 127.0)
        for t in range(tiles):
            row, _ = eighth(t)
            wj[row : row + 1, :] = wide[t : t + 1] * 16.0

    fetch(g, slot).wait()

    @pl.when(g + 1 < groups)
    def _():
        fetch(g + 1, 1 - slot).start()

    x_ref = x_buf.at[slot]
    lengths = jnp.zeros((8, 128), jnp.int32)
    for i in range(8):
        lengths = jnp.where(sub == i, len_ref[(base + g) * 8 + i], lengths)
    left = lengths - lane
    for l in range(levels):
        x = [jnp.where(left > 128 * b, x_ref[l, :, b * 128 : (b + 1) * 128], 0.0) for b in range(blocks)]
        x = jnp.concatenate(x, axis=0)
        hi = x.astype(jnp.bfloat16)
        lo = (x - hi.astype(jnp.float32)).astype(jnp.bfloat16)
        both = jnp.dot(jnp.concatenate([hi, lo], axis=1), fold[...], preferred_element_type=jnp.float32)
        for ref, v in ((xe, both[:, :128]), (xo, both[:, 128:])):
            v = v.reshape(blocks, 8, 128)
            above = [v[middle + i] for i in range(1, middle + 1)]
            below = [v[middle - i] for i in range(1, middle + 1)]
            terms = [v[middle]] + [p + q for p, q in zip(above, below)] + [p - q for p, q in zip(above, below)]
            for b, term in enumerate(terms):
                top = term.astype(jnp.bfloat16).astype(jnp.float32)
                ref[pl.ds(b * 64 + l * 8, 8), :] = jnp.where(low, top, term - top)

    odd = (2 * sub + 1).astype(jnp.float32)

    def prepare(r):
        length = len_ref[(base + g) * 8 + r]
        lf = (jnp.zeros((8, 128), jnp.int32) + length).astype(jnp.float32)
        inv = 1.0 / lf
        two = lf * 2.0
        half = inv * 0.5
        scale = jnp.where(2.0 * wv[...] < lf, inv, 0.0)
        turn = unit(wj[0:8, :], two, half)
        last = unit(wj[8:16, :], two, half)
        steps = (turn, last)
        twice = turn[0] + turn[0]
        turns = [(jnp.ones_like(twice), jnp.zeros_like(twice)), turn]
        for _ in range(middle - 1):
            (c0, s0), (c1, s1) = turns[-2:]
            turns.append((twice * c1 - c0, twice * s1 - s0))
        cz, sz = last[0] * scale, last[1] * scale
        le = xe[pl.ds(r, height, stride=8), :].astype(jnp.bfloat16)
        lo = xo[pl.ds(r, height, stride=8), :].astype(jnp.bfloat16)
        le = jnp.concatenate([le, le], axis=1)
        lo = jnp.concatenate([lo, lo], axis=1)
        return two, half, steps, turns, (cz, sz), le, lo

    def tables(row, t):
        two, half, steps = row[:3]
        at, which = eighth(t)
        step = pick(steps[which][0], at & 7), pick(steps[which][1], at & 7)
        c, s = unit(pick(wv[...], t) * odd, two, half)
        d, e = times((c, s), step)
        cs, ss = [c, d], [s, e]
        twice = step[0] + step[0]
        for _ in range(6):
            cs.append(twice * cs[-1] - cs[-2])
            ss.append(twice * ss[-1] - ss[-2])
        pair = []
        for v in (cs, ss):
            v = jnp.concatenate(v, axis=0)
            top = v.astype(jnp.bfloat16)
            rest = (v - top.astype(jnp.float32)).astype(jnp.bfloat16)
            pair.append(jnp.concatenate([top, top, rest, rest], axis=0))
        return pair

    def multiply(row, ts):
        group = [tables(row, t) for t in ts]
        cos = jnp.concatenate([e[0] for e in group], axis=1)
        sin = jnp.concatenate([e[1] for e in group], axis=1)
        even = jnp.dot(row[5], cos, preferred_element_type=jnp.float32).reshape(blocks, 8, cos.shape[1])
        odds = jnp.dot(row[6], sin, preferred_element_type=jnp.float32).reshape(blocks, 8, cos.shape[1])
        return even, odds

    def gather(row, ts, even, odds):
        out = []
        for i, t in enumerate(ts):
            at = slice(128 * i, 128 * i + 128)
            total = (even[0, :, at], odds[0, :, at])
            for b in range(1, middle + 1):
                c, s = pick(row[3][b][0], t), pick(row[3][b][1], t)
                total = (
                    total[0] + (c * even[b, :, at] - s * odds[middle + b, :, at]),
                    total[1] + (c * odds[b, :, at] + s * even[middle + b, :, at]),
                )
            re, im = times(total, (pick(row[4][0], t), pick(row[4][1], t)))
            out.append((re, -im))
        return out

    def finish(p, first, second):
        r0 = p * 2
        for t in range(tiles):
            for c in range(2):
                u, v = first[t][c], second[t][c]
                even = jnp.where(low, u, pltpu.roll(v, 64, 1))
                odd = jnp.where(low, pltpu.roll(u, 64, 1), v)
                a[p, pl.ds(c * slots + 2 * t, levels, stride=2 * slots), :] = even[:levels]
                a[p, pl.ds(c * slots + 2 * t + 1, levels, stride=2 * slots), :] = odd[:levels]
        turned = a[p].T
        o[pl.ds(g * 8 + r0, 64, stride=rows), :] = turned[:64]
        o[pl.ds(g * 8 + r0 + 1, 64, stride=rows), :] = turned[64:]

    rows_out = [[] for _ in range(8)]
    waiting = []

    def drain():
        r, row, ts, even, odds = waiting.pop(0)
        rows_out[r] += gather(row, ts, even, odds)
        if r % 2 and len(rows_out[r]) == tiles:
            finish(r // 2, rows_out[r - 1], rows_out[r])

    for r in range(8):
        row = prepare(r)
        for t in range(0, tiles, 2):
            ts = list(range(t, min(t + 2, tiles)))
            waiting.append((r, row, ts, *multiply(row, ts)))
            if len(waiting) > LAG:
                drain()
    while waiting:
        drain()

    @pl.when(g == groups - 1)
    def _():
        mine = south_ref[0] * (32 * rows)
        keep_ref[...] = o[pl.ds(pl.multiple_of(mine, 32 * rows), 32 * rows), :]
        give_ref[...] = o[pl.ds(pl.multiple_of(32 * rows - mine, 32 * rows), 32 * rows), :].astype(jnp.bfloat16)


def transform(x, lengths, south, waves, slots, base, groups):
    levels, count, points = x.shape
    rows = 8 * groups
    kernel = functools.partial(dft_kernel, groups, base, levels, slots)
    flops = 2 * 6 * rows * levels * points * 640
    whole = pl.BlockSpec((32 * rows, 128), lambda g: (0, 0))
    return pl.pallas_call(
        kernel,
        grid=(groups,),
        out_shape=(
            jax.ShapeDtypeStruct((32 * rows, 128), jnp.bfloat16),
            jax.ShapeDtypeStruct((32 * rows, 128), jnp.float32),
        ),
        in_specs=[
            pl.BlockSpec(memory_space=pltpu.SMEM),
            pl.BlockSpec(memory_space=pltpu.SMEM),
            pl.BlockSpec((slots // 2, 128), lambda g: (0, 0)),
            pl.BlockSpec(memory_space=pltpu.HBM),
        ],
        out_specs=(whole, whole),
        scratch_shapes=[
            pltpu.VMEM((points // 128 * 64, 128), jnp.float32),
            pltpu.VMEM((points // 128 * 64, 128), jnp.float32),
            pltpu.VMEM((256, 256), jnp.bfloat16),
            pltpu.VMEM((8, 128), jnp.float32),
            pltpu.VMEM((16, 128), jnp.float32),
            pltpu.VMEM((4, 128, 128), jnp.float32),
            pltpu.VMEM((64 * rows, 128), jnp.float32),
            pltpu.VMEM((2, levels, 8, points), jnp.float32),
            pltpu.SemaphoreType.DMA((2,)),
        ],
        compiler_params=pltpu.CompilerParams(vmem_limit_bytes=LIMITS[base > 0] * MIB),
        cost_estimate=pl.CostEstimate(flops=flops, bytes_accessed=rows * levels * points * 4, transcendentals=0),
    )(lengths, south, waves, x)


def fold_kernel(chunks, south_ref, *refs):
    n = len(chunks)
    o_ref = refs[-1]
    sign = 1.0 - 2.0 * south_ref[0].astype(jnp.float32)

    def two_owners(j, _):
        parts = [[], [], [], []]
        for i, (_, groups) in enumerate(chunks):
            rows = 16 * groups
            at = pl.ds(pl.multiple_of(j * rows, rows), rows)
            other = refs[i][at, :].astype(jnp.float32)
            mine = refs[n + i][at, :]
            plus = mine + other
            minus = (mine - other) * sign
            for k in range(2):
                parts[2 * k].append(plus[k * rows // 2 : (k + 1) * rows // 2])
                parts[2 * k + 1].append(minus[k * rows // 2 : (k + 1) * rows // 2])
        block = jnp.concatenate([e for part in parts for e in part], axis=0)
        size = block.shape[0]
        o_ref[pl.ds(pl.multiple_of(j * size, size), size), :] = block.astype(jnp.bfloat16)
        return 0

    lax.fori_loop(0, 16, two_owners, 0, unroll=2)


def folded(others, mine, south, chunks):
    total = sum(8 * groups for _, groups in chunks)
    vmem = pl.BlockSpec(memory_space=pltpu.VMEM)
    return pl.pallas_call(
        functools.partial(fold_kernel, chunks),
        out_shape=jax.ShapeDtypeStruct((64 * total, 128), jnp.bfloat16),
        in_specs=[pl.BlockSpec(memory_space=pltpu.SMEM)] + [vmem] * (2 * len(chunks)),
        out_specs=vmem,
        compiler_params=pltpu.CompilerParams(vmem_limit_bytes=16 * MIB),
        cost_estimate=pl.CostEstimate(flops=64 * total * 256, bytes_accessed=0, transcendentals=0),
    )(south, *others, *mine)


def load_kernel(hbm, after, vmem, sem):
    copy = pltpu.make_async_copy(hbm, vmem, sem)
    copy.start()
    copy.wait()


def load(array, after):
    return pl.pallas_call(
        load_kernel,
        out_shape=jax.ShapeDtypeStruct(array.shape, array.dtype),
        in_specs=[pl.BlockSpec(memory_space=pltpu.HBM), pl.BlockSpec(memory_space=pl.ANY)],
        out_specs=pl.BlockSpec(memory_space=pltpu.VMEM),
        scratch_shapes=[pltpu.SemaphoreType.DMA],
        compiler_params=pltpu.CompilerParams(vmem_limit_bytes=16 * MIB),
        cost_estimate=pl.CostEstimate(flops=0, bytes_accessed=array.size * 2, transcendentals=0),
    )(array, after)


def legendre_kernel(levels, slots, half_ref, place_ref, *refs):
    fields = len(refs) - 4
    parts = refs[:fields]
    leg_ref, kept_ref, given_ref, xt = refs[fields:]
    total = parts[0].shape[0]
    width = 2 * levels * slots
    for i, part in enumerate(parts):
        at = pl.multiple_of(place_ref[i] * width, 8)
        for k in range(0, total, 128):
            xt[k // 128, pl.ds(at, width), :] = part[pl.ds(k, 128), :].astype(jnp.float32).T[:width]
    here = half_ref[0] == 0
    tall = fields * 2 * levels

    for s in range(slots):
        lhs = jnp.concatenate([xt[k, pl.ds(s, tall, stride=slots), :] for k in range(total // 128)], axis=1)
        res = jnp.dot(lhs.astype(jnp.bfloat16), leg_ref[s], preferred_element_type=jnp.float32)
        upper, lower = res[: tall // 2], res[tall // 2 :]
        kept_ref[s] = jnp.where(here, upper, lower)
        given_ref[s] = jnp.where(here, lower, upper).astype(given_ref.dtype)


def project(parts, legendre, half, places, levels, slots):
    _, total, coeffs = legendre.shape
    fields = len(parts)
    width = 2 * levels * slots
    tall = fields * 2 * levels
    vmem = pl.BlockSpec(memory_space=pltpu.VMEM)
    smem = pl.BlockSpec(memory_space=pltpu.SMEM)
    return pl.pallas_call(
        functools.partial(legendre_kernel, levels, slots),
        out_shape=(
            jax.ShapeDtypeStruct((slots, tall // 2, coeffs), jnp.float32),
            jax.ShapeDtypeStruct((slots, tall // 2, coeffs), PARTIAL),
        ),
        in_specs=[smem, smem] + [vmem] * (fields + 1),
        out_specs=(vmem, vmem),
        scratch_shapes=[pltpu.VMEM((total // 128, fields * width, 128), jnp.float32)],
        compiler_params=pltpu.CompilerParams(vmem_limit_bytes=24 * MIB),
        cost_estimate=pl.CostEstimate(flops=4 * slots * tall * total * coeffs, bytes_accessed=slots * total * coeffs * 2, transcendentals=0),
    )(half, places, *parts, legendre)


CHUNKS = ((0, 3), (3, 2))
PARTIAL = jnp.bfloat16
LIMITS = (60, 20)
LAG = 1


def body(grid_fields, row_points, wave_order, legendre, helmholtz_tau):
    lat_count = lax.axis_size("lat")
    fld_count = lax.axis_size("fld")
    lat_index = lax.axis_index("lat")
    fld_index = lax.axis_index("fld")
    count, levels, _ = grid_fields.shape
    slots, total, coeffs = legendre.shape
    owners = lat_count // 2
    x = jnp.transpose(grid_fields, (1, 0, 2))
    waves = wave_order.reshape((slots // 2, 128))
    south = (lat_index // owners).astype(jnp.int32).reshape((1,))
    across = [(i, i ^ owners) for i in range(lat_count)]
    sides = [list(range(owners)), list(range(owners, 2 * owners))]
    others, mine = [], []
    for base, groups in CHUNKS:
        give, keep = transform(x, row_points, south, waves, slots, base, groups)
        others.append(lax.ppermute(give, "lat", across))
        mine.append(keep)
    outgoing = folded(others, mine, south, CHUNKS)
    arrived = lax.all_to_all(outgoing, "lat", split_axis=0, concat_axis=0, tiled=True, axis_index_groups=sides)
    legendre = load(legendre, outgoing)
    arrived = arrived.reshape((2, owners // 2, 2, count, 128)).transpose((2, 0, 1, 3, 4)).reshape((fld_count, total, 128))
    parts, places = [], []
    for k in (0, 2, 1, 3):
        block = lax.dynamic_index_in_dim(arrived, fld_index ^ k, 0, keepdims=False)
        if k:
            block = lax.ppermute(block, "fld", [(i, i ^ k) for i in range(fld_count)])
        parts.append(block)
        places.append(fld_index ^ k)
    places = jnp.stack(places).astype(jnp.int32)
    parity = fld_index // 2
    half = fld_index % 2
    kept, given = project(parts, legendre, half.astype(jnp.int32).reshape((1,)), places, levels, slots)
    combined = kept + lax.ppermute(given, "fld", [(i, i ^ 1) for i in range(fld_count)]).astype(jnp.float32)
    half_levels = levels * fld_count // 2
    owned = lax.dynamic_slice_in_dim(wave_order, lat_index * slots, slots)
    degree = owned[:, None] + 2 * jnp.arange(coeffs, dtype=jnp.int32)[None, :] + parity
    degree = degree.astype(jnp.float32)
    shape_term = degree * (degree + 1.0) / float((2 * coeffs) ** 2)
    rates = lax.dynamic_slice_in_dim(helmholtz_tau, half * half_levels, half_levels)
    operator = 1.0 + rates[None, :, None, None] * shape_term[:, None, None, :]
    return combined.reshape((slots, half_levels, 2, coeffs)) / operator


def solution(mesh):
    in_specs = (P("lat", "fld", None), P("lat"), P(), P("lat", "fld", None), P())
    out_specs = P("lat", "fld", None, None)
    return jax.shard_map(body, mesh=mesh, in_specs=in_specs, out_specs=out_specs, check_vma=False)
```

```python
import functools

import jax
import jax.numpy as jnp
from jax import lax
from jax.experimental import pallas as pl
from jax.experimental.pallas import tpu as pltpu
from jax.sharding import PartitionSpec as P

SIN = (6.283184916495431, -41.341589232688555, 81.59994332978103, -76.61447253122742, 41.34288235446962, -12.471243534881289)
COS = (0.9999999890590217, -19.73920449945379, 64.93911745989134, -85.45013953081433, 60.16763095040022, -25.96759924640718, 6.528658158395448)
MAGIC = 12582912.0
MIB = 1024 * 1024


def horner(coefs, x):
    acc = jnp.full_like(x, coefs[-1])
    for c in coefs[-2::-1]:
        acc = acc * x + c
    return acc


def unit(product, length, inverse):
    turns = (product * inverse + MAGIC) - MAGIC
    u = (product - turns * length) * inverse
    v = u * u
    return horner(COS, v), horner(SIN, v) * u


def times(p, q):
    return p[0] * q[0] - p[1] * q[1], p[1] * q[0] + p[0] * q[1]


def pick(v, t):
    return jnp.broadcast_to(v[t : t + 1], (8, 128))


def dft_kernel(groups, base, levels, slots, len_ref, south_ref, wave_ref, x_hbm, give_ref, keep_ref, xe, xo, xe_next, xo_next, fold, wv, wj, a, o, x_buf, x_sem):
    blocks = x_hbm.shape[2] // 128

    def eighth(t):
        return (tiles + t, 0) if tiles + t < 8 else (2 * tiles + t, 1)

    def fetch(i):
        at = pl.ds((base + i) * 8, 8)
        return pltpu.make_async_copy(x_hbm.at[:, at, :], x_buf.at[i % 2], x_sem.at[i % 2])

    tiles = slots // 2
    rows = 8 * groups
    height = blocks * 8
    middle = blocks // 2
    lane = lax.broadcasted_iota(jnp.int32, (8, 128), 1)
    sub = lax.broadcasted_iota(jnp.int32, (8, 128), 0)
    low = lane < 64

    for i in range(min(groups, 2)):
        fetch(i).start()
    for ref in (xe, xo, xe_next, xo_next):
        for b in range(blocks):
            ref[pl.ds(b * 64 + levels * 8, 64 - levels * 8), :] = jnp.zeros((64 - levels * 8, 128), jnp.float32)
    a[...] = jnp.zeros_like(a)
    point = lax.broadcasted_iota(jnp.int32, (256, 256), 0) & 127
    column = lax.broadcasted_iota(jnp.int32, (256, 256), 1)
    k = column & 63
    plus = jnp.where(point == 64 + k, 1.0, 0.0)
    minus = jnp.where(point == 63 - k, 1.0, 0.0)
    fold[...] = jnp.where(column < 128, plus + minus, plus - minus).astype(jnp.bfloat16)
    order = wave_ref[...]
    order = jnp.concatenate([order >> 5, order & 31], axis=0).astype(jnp.float32).astype(jnp.bfloat16)
    source = lax.broadcasted_iota(jnp.int32, (128, 128), 0)
    target = lax.broadcasted_iota(jnp.int32, (128, 128), 1)
    wv[...] = jnp.zeros_like(wv)
    for t in range(tiles):
        index = (target & 63) * slots + 2 * t + (target >> 6)
        chosen = jnp.where((index & 127) == source, 1.0, 0.0).astype(jnp.bfloat16)
        found = jnp.dot(order, chosen, preferred_element_type=jnp.float32)
        found = found[:tiles] * 32.0 + found[tiles:]
        here = (index[:tiles] >> 7) == source[:tiles]
        wv[t : t + 1, :] = jnp.sum(jnp.where(here, found, 0.0), axis=0, keepdims=True)
    wide = wv[...]
    wj[0:8, :] = wide * 256.0
    wj[8:16, :] = wide * (256.0 * middle + 127.0)
    for t in range(tiles):
        row, _ = eighth(t)
        wj[row : row + 1, :] = wide[t : t + 1] * 16.0

    def split(step, even_ref, odd_ref):
        x_ref = x_buf.at[step % 2]
        lengths = jnp.zeros((8, 128), jnp.int32)
        for i in range(8):
            lengths = jnp.where(sub == i, len_ref[(base + step) * 8 + i], lengths)
        left = lengths - lane
        for l in range(levels):
            x = [jnp.where(left > 128 * b, x_ref[l, :, b * 128 : (b + 1) * 128], 0.0) for b in range(blocks)]
            x = jnp.concatenate(x, axis=0)
            hi = x.astype(jnp.bfloat16)
            lo = (x - hi.astype(jnp.float32)).astype(jnp.bfloat16)
            both = jnp.dot(jnp.concatenate([hi, lo], axis=1), fold[...], preferred_element_type=jnp.float32)
            for ref, v in ((even_ref, both[:, :128]), (odd_ref, both[:, 128:])):
                v = v.reshape(blocks, 8, 128)
                above = [v[middle + i] for i in range(1, middle + 1)]
                below = [v[middle - i] for i in range(1, middle + 1)]
                terms = [v[middle]] + [p + q for p, q in zip(above, below)] + [p - q for p, q in zip(above, below)]
                for b, term in enumerate(terms):
                    top = term.astype(jnp.bfloat16).astype(jnp.float32)
                    ref[pl.ds(b * 64 + l * 8, 8), :] = jnp.where(low, top, term - top)

    odd = (2 * sub + 1).astype(jnp.float32)

    def prepare(g, r, xe, xo):
        length = len_ref[(base + g) * 8 + r]
        lf = (jnp.zeros((8, 128), jnp.int32) + length).astype(jnp.float32)
        inv = 1.0 / lf
        two = lf * 2.0
        half = inv * 0.5
        scale = jnp.where(2.0 * wv[...] < lf, inv, 0.0)
        turn = unit(wj[0:8, :], two, half)
        last = unit(wj[8:16, :], two, half)
        steps = (turn, last)
        twice = turn[0] + turn[0]
        turns = [(jnp.ones_like(twice), jnp.zeros_like(twice)), turn]
        for _ in range(middle - 1):
            (c0, s0), (c1, s1) = turns[-2:]
            turns.append((twice * c1 - c0, twice * s1 - s0))
        cz, sz = last[0] * scale, last[1] * scale
        le = xe[pl.ds(r, height, stride=8), :].astype(jnp.bfloat16)
        lo = xo[pl.ds(r, height, stride=8), :].astype(jnp.bfloat16)
        le = jnp.concatenate([le, le], axis=1)
        lo = jnp.concatenate([lo, lo], axis=1)
        return two, half, steps, turns, (cz, sz), le, lo

    def tables(row, t):
        two, half, steps = row[:3]
        at, which = eighth(t)
        step = pick(steps[which][0], at & 7), pick(steps[which][1], at & 7)
        c, s = unit(pick(wv[...], t) * odd, two, half)
        d, e = times((c, s), step)
        cs, ss = [c, d], [s, e]
        twice = step[0] + step[0]
        for _ in range(6):
            cs.append(twice * cs[-1] - cs[-2])
            ss.append(twice * ss[-1] - ss[-2])
        pair = []
        for v in (cs, ss):
            v = jnp.concatenate(v, axis=0)
            top = v.astype(jnp.bfloat16)
            rest = (v - top.astype(jnp.float32)).astype(jnp.bfloat16)
            pair.append(jnp.concatenate([top, top, rest, rest], axis=0))
        return pair

    def multiply(row, ts):
        group = [tables(row, t) for t in ts]
        cos = jnp.concatenate([e[0] for e in group], axis=1)
        sin = jnp.concatenate([e[1] for e in group], axis=1)
        even = jnp.dot(row[5], cos, preferred_element_type=jnp.float32).reshape(blocks, 8, cos.shape[1])
        odds = jnp.dot(row[6], sin, preferred_element_type=jnp.float32).reshape(blocks, 8, cos.shape[1])
        return even, odds

    def gather(row, ts, even, odds):
        out = []
        for i, t in enumerate(ts):
            at = slice(128 * i, 128 * i + 128)
            total = (even[0, :, at], odds[0, :, at])
            for b in range(1, middle + 1):
                c, s = pick(row[3][b][0], t), pick(row[3][b][1], t)
                total = (
                    total[0] + (c * even[b, :, at] - s * odds[middle + b, :, at]),
                    total[1] + (c * odds[b, :, at] + s * even[middle + b, :, at]),
                )
            re, im = times(total, (pick(row[4][0], t), pick(row[4][1], t)))
            out.append((re, -im))
        return out

    def finish(g, p, first, second):
        r0 = p * 2
        for t in range(tiles):
            for c in range(2):
                u, v = first[t][c], second[t][c]
                even = jnp.where(low, u, pltpu.roll(v, 64, 1))
                odd = jnp.where(low, pltpu.roll(u, 64, 1), v)
                a[p, pl.ds(c * slots + 2 * t, levels, stride=2 * slots), :] = even[:levels]
                a[p, pl.ds(c * slots + 2 * t + 1, levels, stride=2 * slots), :] = odd[:levels]
        turned = a[p].T
        o[pl.ds(g * 8 + r0, 64, stride=rows), :] = turned[:64]
        o[pl.ds(g * 8 + r0 + 1, 64, stride=rows), :] = turned[64:]

    sides = ((xe, xo), (xe_next, xo_next))
    fetch(0).wait()
    split(0, *sides[0])
    results = {}
    waiting = []

    def drain():
        g, r, row, ts, even, odds = waiting.pop(0)
        out = results.setdefault((g, r), [])
        out += gather(row, ts, even, odds)
        if r % 2 and len(out) == tiles:
            finish(g, r // 2, results[g, r - 1], out)

    for g in range(groups):
        if g + 1 < groups:
            fetch(g + 1).wait()
        if g + 2 < groups:
            fetch(g + 2).start()
        for r in range(8):
            if r == SPLIT_AT and g + 1 < groups:
                split(g + 1, *sides[(g + 1) % 2])
            row = prepare(g, r, *sides[g % 2])
            for t in range(0, tiles, 2):
                ts = list(range(t, min(t + 2, tiles)))
                waiting.append((g, r, row, ts, *multiply(row, ts)))
                if len(waiting) > LAG:
                    drain()
    while waiting:
        drain()

    mine = south_ref[0] * (32 * rows)
    keep_ref[...] = o[pl.ds(pl.multiple_of(mine, 32 * rows), 32 * rows), :]
    give_ref[...] = o[pl.ds(pl.multiple_of(32 * rows - mine, 32 * rows), 32 * rows), :].astype(jnp.bfloat16)


def transform(x, lengths, south, waves, slots, base, groups):
    levels, count, points = x.shape
    rows = 8 * groups
    kernel = functools.partial(dft_kernel, groups, base, levels, slots)
    flops = 2 * 6 * rows * levels * points * 640
    whole = pl.BlockSpec((32 * rows, 128), lambda g: (0, 0))
    return pl.pallas_call(
        kernel,
        grid=(1,),
        out_shape=(
            jax.ShapeDtypeStruct((32 * rows, 128), jnp.bfloat16),
            jax.ShapeDtypeStruct((32 * rows, 128), jnp.float32),
        ),
        in_specs=[
            pl.BlockSpec(memory_space=pltpu.SMEM),
            pl.BlockSpec(memory_space=pltpu.SMEM),
            pl.BlockSpec((slots // 2, 128), lambda g: (0, 0)),
            pl.BlockSpec(memory_space=pltpu.HBM),
        ],
        out_specs=(whole, whole),
        scratch_shapes=[
            pltpu.VMEM((points // 128 * 64, 128), jnp.float32),
            pltpu.VMEM((points // 128 * 64, 128), jnp.float32),
            pltpu.VMEM((points // 128 * 64, 128), jnp.float32),
            pltpu.VMEM((points // 128 * 64, 128), jnp.float32),
            pltpu.VMEM((256, 256), jnp.bfloat16),
            pltpu.VMEM((8, 128), jnp.float32),
            pltpu.VMEM((16, 128), jnp.float32),
            pltpu.VMEM((4, 128, 128), jnp.float32),
            pltpu.VMEM((64 * rows, 128), jnp.float32),
            pltpu.VMEM((2, levels, 8, points), jnp.float32),
            pltpu.SemaphoreType.DMA((2,)),
        ],
        compiler_params=pltpu.CompilerParams(vmem_limit_bytes=LIMITS[base > 0] * MIB),
        cost_estimate=pl.CostEstimate(flops=flops, bytes_accessed=rows * levels * points * 4, transcendentals=0),
    )(lengths, south, waves, x)


def fold_kernel(chunks, south_ref, *refs):
    n = len(chunks)
    o_ref = refs[-1]
    sign = 1.0 - 2.0 * south_ref[0].astype(jnp.float32)

    def two_owners(j, _):
        parts = [[], [], [], []]
        for i, (_, groups) in enumerate(chunks):
            rows = 16 * groups
            at = pl.ds(pl.multiple_of(j * rows, rows), rows)
            other = refs[i][at, :].astype(jnp.float32)
            mine = refs[n + i][at, :]
            plus = mine + other
            minus = (mine - other) * sign
            for k in range(2):
                parts[2 * k].append(plus[k * rows // 2 : (k + 1) * rows // 2])
                parts[2 * k + 1].append(minus[k * rows // 2 : (k + 1) * rows // 2])
        block = jnp.concatenate([e for part in parts for e in part], axis=0)
        size = block.shape[0]
        o_ref[pl.ds(pl.multiple_of(j * size, size), size), :] = block.astype(jnp.bfloat16)
        return 0

    lax.fori_loop(0, 16, two_owners, 0, unroll=4)


def folded(others, mine, south, chunks):
    total = sum(8 * groups for _, groups in chunks)
    vmem = pl.BlockSpec(memory_space=pltpu.VMEM)
    return pl.pallas_call(
        functools.partial(fold_kernel, chunks),
        out_shape=jax.ShapeDtypeStruct((64 * total, 128), jnp.bfloat16),
        in_specs=[pl.BlockSpec(memory_space=pltpu.SMEM)] + [vmem] * (2 * len(chunks)),
        out_specs=vmem,
        compiler_params=pltpu.CompilerParams(vmem_limit_bytes=16 * MIB),
        cost_estimate=pl.CostEstimate(flops=64 * total * 256, bytes_accessed=0, transcendentals=0),
    )(south, *others, *mine)


def load_kernel(hbm, after, vmem, sem):
    copy = pltpu.make_async_copy(hbm, vmem, sem)
    copy.start()
    copy.wait()


def load(array, after):
    return pl.pallas_call(
        load_kernel,
        out_shape=jax.ShapeDtypeStruct(array.shape, array.dtype),
        in_specs=[pl.BlockSpec(memory_space=pltpu.HBM), pl.BlockSpec(memory_space=pl.ANY)],
        out_specs=pl.BlockSpec(memory_space=pltpu.VMEM),
        scratch_shapes=[pltpu.SemaphoreType.DMA],
        compiler_params=pltpu.CompilerParams(vmem_limit_bytes=16 * MIB),
        cost_estimate=pl.CostEstimate(flops=0, bytes_accessed=array.size * 2, transcendentals=0),
    )(array, after)


def legendre_kernel(levels, slots, half_ref, place_ref, *refs):
    fields = len(refs) - 4
    parts = refs[:fields]
    leg_ref, kept_ref, given_ref, xt = refs[fields:]
    total = parts[0].shape[0]
    width = 2 * levels * slots
    for i, part in enumerate(parts):
        at = pl.multiple_of(place_ref[i] * width, 8)
        for k in range(0, total, 128):
            xt[k // 128, pl.ds(at, width), :] = part[pl.ds(k, 128), :].astype(jnp.float32).T[:width]
    here = half_ref[0] == 0
    tall = fields * 2 * levels

    for s in range(slots):
        lhs = jnp.concatenate([xt[k, pl.ds(s, tall, stride=slots), :] for k in range(total // 128)], axis=1)
        res = jnp.dot(lhs.astype(jnp.bfloat16), leg_ref[s], preferred_element_type=jnp.float32)
        upper, lower = res[: tall // 2], res[tall // 2 :]
        kept_ref[s] = jnp.where(here, upper, lower)
        given_ref[s] = jnp.where(here, lower, upper).astype(given_ref.dtype)


def project(parts, legendre, half, places, levels, slots):
    _, total, coeffs = legendre.shape
    fields = len(parts)
    width = 2 * levels * slots
    tall = fields * 2 * levels
    vmem = pl.BlockSpec(memory_space=pltpu.VMEM)
    smem = pl.BlockSpec(memory_space=pltpu.SMEM)
    return pl.pallas_call(
        functools.partial(legendre_kernel, levels, slots),
        out_shape=(
            jax.ShapeDtypeStruct((slots, tall // 2, coeffs), jnp.float32),
            jax.ShapeDtypeStruct((slots, tall // 2, coeffs), PARTIAL),
        ),
        in_specs=[smem, smem] + [vmem] * (fields + 1),
        out_specs=(vmem, vmem),
        scratch_shapes=[pltpu.VMEM((total // 128, fields * width, 128), jnp.float32)],
        compiler_params=pltpu.CompilerParams(vmem_limit_bytes=24 * MIB),
        cost_estimate=pl.CostEstimate(flops=4 * slots * tall * total * coeffs, bytes_accessed=slots * total * coeffs * 2, transcendentals=0),
    )(half, places, *parts, legendre)


CHUNKS = ((0, 3), (3, 2))
PARTIAL = jnp.bfloat16
LIMITS = (60, 20)
LAG = 1
SPLIT_AT = 4


def body(grid_fields, row_points, wave_order, legendre, helmholtz_tau):
    lat_count = lax.axis_size("lat")
    fld_count = lax.axis_size("fld")
    lat_index = lax.axis_index("lat")
    fld_index = lax.axis_index("fld")
    count, levels, _ = grid_fields.shape
    slots, total, coeffs = legendre.shape
    owners = lat_count // 2
    x = jnp.transpose(grid_fields, (1, 0, 2))
    waves = wave_order.reshape((slots // 2, 128))
    south = (lat_index // owners).astype(jnp.int32).reshape((1,))
    across = [(i, i ^ owners) for i in range(lat_count)]
    sides = [list(range(owners)), list(range(owners, 2 * owners))]
    others, mine = [], []
    for base, groups in CHUNKS:
        give, keep = transform(x, row_points, south, waves, slots, base, groups)
        others.append(lax.ppermute(give, "lat", across))
        mine.append(keep)
    outgoing = folded(others, mine, south, CHUNKS)
    arrived = lax.all_to_all(outgoing, "lat", split_axis=0, concat_axis=0, tiled=True, axis_index_groups=sides)
    legendre = load(legendre, outgoing)
    arrived = arrived.reshape((2, owners // 2, 2, count, 128)).transpose((2, 0, 1, 3, 4)).reshape((fld_count, total, 128))
    parts, places = [], []
    for k in (0, 2, 1, 3):
        block = lax.dynamic_index_in_dim(arrived, fld_index ^ k, 0, keepdims=False)
        if k:
            block = lax.ppermute(block, "fld", [(i, i ^ k) for i in range(fld_count)])
        parts.append(block)
        places.append(fld_index ^ k)
    places = jnp.stack(places).astype(jnp.int32)
    parity = fld_index // 2
    half = fld_index % 2
    kept, given = project(parts, legendre, half.astype(jnp.int32).reshape((1,)), places, levels, slots)
    combined = kept + lax.ppermute(given, "fld", [(i, i ^ 1) for i in range(fld_count)]).astype(jnp.float32)
    half_levels = levels * fld_count // 2
    owned = lax.dynamic_slice_in_dim(wave_order, lat_index * slots, slots)
    degree = owned[:, None] + 2 * jnp.arange(coeffs, dtype=jnp.int32)[None, :] + parity
    degree = degree.astype(jnp.float32)
    shape_term = degree * (degree + 1.0) / float((2 * coeffs) ** 2)
    rates = lax.dynamic_slice_in_dim(helmholtz_tau, half * half_levels, half_levels)
    operator = 1.0 + rates[None, :, None, None] * shape_term[:, None, None, :]
    return combined.reshape((slots, half_levels, 2, coeffs)) / operator


def solution(mesh):
    in_specs = (P("lat", "fld", None), P("lat"), P(), P("lat", "fld", None), P())
    out_specs = P("lat", "fld", None, None)
    return jax.shard_map(body, mesh=mesh, in_specs=in_specs, out_specs=out_specs, check_vma=False)
```

```python
import functools

import jax
import jax.numpy as jnp
from jax import lax
from jax.experimental import pallas as pl
from jax.experimental.pallas import tpu as pltpu
from jax.sharding import PartitionSpec as P

SIN = (6.283184916495431, -41.341589232688555, 81.59994332978103, -76.61447253122742, 41.34288235446962, -12.471243534881289)
COS = (0.9999999890590217, -19.73920449945379, 64.93911745989134, -85.45013953081433, 60.16763095040022, -25.96759924640718, 6.528658158395448)
MAGIC = 12582912.0
MIB = 1024 * 1024


def horner(coefs, x):
    acc = jnp.full_like(x, coefs[-1])
    for c in coefs[-2::-1]:
        acc = acc * x + c
    return acc


def unit(product, length, inverse):
    turns = (product * inverse + MAGIC) - MAGIC
    u = (product - turns * length) * inverse
    v = u * u
    return horner(COS, v), horner(SIN, v) * u


def times(p, q):
    return p[0] * q[0] - p[1] * q[1], p[1] * q[0] + p[0] * q[1]


def pick(v, t):
    return jnp.broadcast_to(v[t : t + 1], (8, 128))


def dft_kernel(groups, base, levels, slots, len_ref, south_ref, wave_ref, x_hbm, give_ref, keep_ref, xe, xo, xe_next, xo_next, fold, wv, wj, a, o, x_buf, x_sem):
    blocks = x_hbm.shape[2] // 128

    def eighth(t):
        return (tiles + t, 0) if tiles + t < 8 else (2 * tiles + t, 1)

    def fetch(i):
        at = pl.ds((base + i) * 8, 8)
        return pltpu.make_async_copy(x_hbm.at[:, at, :], x_buf.at[i % 2], x_sem.at[i % 2])

    tiles = slots // 2
    rows = 8 * groups
    height = blocks * 8
    middle = blocks // 2
    lane = lax.broadcasted_iota(jnp.int32, (8, 128), 1)
    sub = lax.broadcasted_iota(jnp.int32, (8, 128), 0)
    low = lane < 64

    for i in range(min(groups, 2)):
        fetch(i).start()
    for ref in (xe, xo, xe_next, xo_next):
        for b in range(blocks):
            ref[pl.ds(b * 64 + levels * 8, 64 - levels * 8), :] = jnp.zeros((64 - levels * 8, 128), jnp.float32)
    a[...] = jnp.zeros_like(a)
    point = lax.broadcasted_iota(jnp.int32, (256, 256), 0) & 127
    column = lax.broadcasted_iota(jnp.int32, (256, 256), 1)
    k = column & 63
    plus = jnp.where(point == 64 + k, 1.0, 0.0)
    minus = jnp.where(point == 63 - k, 1.0, 0.0)
    fold[...] = jnp.where(column < 128, plus + minus, plus - minus).astype(jnp.bfloat16)
    order = wave_ref[...]
    order = jnp.concatenate([order >> 5, order & 31], axis=0).astype(jnp.float32).astype(jnp.bfloat16)
    source = lax.broadcasted_iota(jnp.int32, (128, 128), 0)
    target = lax.broadcasted_iota(jnp.int32, (128, 128), 1)
    wv[...] = jnp.zeros_like(wv)
    for t in range(tiles):
        index = (target & 63) * slots + 2 * t + (target >> 6)
        chosen = jnp.where((index & 127) == source, 1.0, 0.0).astype(jnp.bfloat16)
        found = jnp.dot(order, chosen, preferred_element_type=jnp.float32)
        found = found[:tiles] * 32.0 + found[tiles:]
        here = (index[:tiles] >> 7) == source[:tiles]
        wv[t : t + 1, :] = jnp.sum(jnp.where(here, found, 0.0), axis=0, keepdims=True)
    wide = wv[...]
    wj[0:8, :] = wide * 256.0
    wj[8:16, :] = wide * (256.0 * middle + 127.0)
    for t in range(tiles):
        row, _ = eighth(t)
        wj[row : row + 1, :] = wide[t : t + 1] * 16.0

    def split(step, even_ref, odd_ref):
        x_ref = x_buf.at[step % 2]
        lengths = jnp.zeros((8, 128), jnp.int32)
        for i in range(8):
            lengths = jnp.where(sub == i, len_ref[(base + step) * 8 + i], lengths)
        left = lengths - lane
        for l in range(levels):
            x = [jnp.where(left > 128 * b, x_ref[l, :, b * 128 : (b + 1) * 128], 0.0) for b in range(blocks)]
            x = jnp.concatenate(x, axis=0)
            hi = x.astype(jnp.bfloat16)
            lo = (x - hi.astype(jnp.float32)).astype(jnp.bfloat16)
            both = jnp.dot(jnp.concatenate([hi, lo], axis=1), fold[...], preferred_element_type=jnp.float32)
            for ref, v in ((even_ref, both[:, :128]), (odd_ref, both[:, 128:])):
                v = v.reshape(blocks, 8, 128)
                above = [v[middle + i] for i in range(1, middle + 1)]
                below = [v[middle - i] for i in range(1, middle + 1)]
                terms = [v[middle]] + [p + q for p, q in zip(above, below)] + [p - q for p, q in zip(above, below)]
                for b, term in enumerate(terms):
                    top = term.astype(jnp.bfloat16).astype(jnp.float32)
                    ref[pl.ds(b * 64 + l * 8, 8), :] = jnp.where(low, top, term - top)

    odd = (2 * sub + 1).astype(jnp.float32)

    def prepare(g, r, xe, xo):
        length = len_ref[(base + g) * 8 + r]
        lf = (jnp.zeros((8, 128), jnp.int32) + length).astype(jnp.float32)
        inv = 1.0 / lf
        two = lf * 2.0
        half = inv * 0.5
        scale = jnp.where(2.0 * wv[...] < lf, inv, 0.0)
        turn = unit(wj[0:8, :], two, half)
        last = unit(wj[8:16, :], two, half)
        steps = (turn, last)
        twice = turn[0] + turn[0]
        turns = [(jnp.ones_like(twice), jnp.zeros_like(twice)), turn]
        for _ in range(middle - 1):
            (c0, s0), (c1, s1) = turns[-2:]
            turns.append((twice * c1 - c0, twice * s1 - s0))
        cz, sz = last[0] * scale, last[1] * scale
        le = xe[pl.ds(r, height, stride=8), :].astype(jnp.bfloat16)
        lo = xo[pl.ds(r, height, stride=8), :].astype(jnp.bfloat16)
        le = jnp.concatenate([le, le], axis=1)
        lo = jnp.concatenate([lo, lo], axis=1)
        return two, half, steps, turns, (cz, sz), le, lo

    def tables(row, t):
        two, half, steps = row[:3]
        at, which = eighth(t)
        step = pick(steps[which][0], at & 7), pick(steps[which][1], at & 7)
        c, s = unit(pick(wv[...], t) * odd, two, half)
        d, e = times((c, s), step)
        cs, ss = [c, d], [s, e]
        twice = step[0] + step[0]
        for _ in range(6):
            cs.append(twice * cs[-1] - cs[-2])
            ss.append(twice * ss[-1] - ss[-2])
        pair = []
        for v in (cs, ss):
            v = jnp.concatenate(v, axis=0)
            top = v.astype(jnp.bfloat16)
            rest = (v - top.astype(jnp.float32)).astype(jnp.bfloat16)
            pair.append(jnp.concatenate([top, top, rest, rest], axis=0))
        return pair

    def multiply(row, ts):
        group = [tables(row, t) for t in ts]
        cos = jnp.concatenate([e[0] for e in group], axis=1)
        sin = jnp.concatenate([e[1] for e in group], axis=1)
        even = jnp.dot(row[5], cos, preferred_element_type=jnp.float32).reshape(blocks, 8, cos.shape[1])
        odds = jnp.dot(row[6], sin, preferred_element_type=jnp.float32).reshape(blocks, 8, cos.shape[1])
        return even, odds

    def gather(row, ts, even, odds):
        out = []
        for i, t in enumerate(ts):
            at = slice(128 * i, 128 * i + 128)
            total = (even[0, :, at], odds[0, :, at])
            for b in range(1, middle + 1):
                c, s = pick(row[3][b][0], t), pick(row[3][b][1], t)
                total = (
                    total[0] + (c * even[b, :, at] - s * odds[middle + b, :, at]),
                    total[1] + (c * odds[b, :, at] + s * even[middle + b, :, at]),
                )
            re, im = times(total, (pick(row[4][0], t), pick(row[4][1], t)))
            out.append((re, -im))
        return out

    def finish(g, p, first, second):
        r0 = p * 2
        for t in range(tiles):
            for c in range(2):
                u, v = first[t][c], second[t][c]
                even = jnp.where(low, u, pltpu.roll(v, 64, 1))
                odd = jnp.where(low, pltpu.roll(u, 64, 1), v)
                a[p, pl.ds(c * slots + 2 * t, levels, stride=2 * slots), :] = even[:levels]
                a[p, pl.ds(c * slots + 2 * t + 1, levels, stride=2 * slots), :] = odd[:levels]
        turned = a[p].T
        o[pl.ds(g * 8 + r0, 64, stride=rows), :] = turned[:64]
        o[pl.ds(g * 8 + r0 + 1, 64, stride=rows), :] = turned[64:]

    sides = ((xe, xo), (xe_next, xo_next))
    fetch(0).wait()
    split(0, *sides[0])
    results = {}
    waiting = []

    def drain():
        g, r, row, ts, even, odds = waiting.pop(0)
        out = results.setdefault((g, r), [])
        out += gather(row, ts, even, odds)
        if r % 2 and len(out) == tiles:
            finish(g, r // 2, results[g, r - 1], out)

    for g in range(groups):
        if g + 1 < groups:
            fetch(g + 1).wait()
        if g + 2 < groups:
            fetch(g + 2).start()
        for r in range(8):
            if r == SPLIT_AT and g + 1 < groups:
                split(g + 1, *sides[(g + 1) % 2])
            row = prepare(g, r, *sides[g % 2])
            for t in range(0, tiles, 2):
                ts = list(range(t, min(t + 2, tiles)))
                waiting.append((g, r, row, ts, *multiply(row, ts)))
                if len(waiting) > LAG:
                    drain()
    while waiting:
        drain()

    mine = south_ref[0] * (32 * rows)
    keep_ref[...] = o[pl.ds(pl.multiple_of(mine, 32 * rows), 32 * rows), :]
    give_ref[...] = o[pl.ds(pl.multiple_of(32 * rows - mine, 32 * rows), 32 * rows), :].astype(jnp.bfloat16)


def transform(x, lengths, south, waves, slots, base, groups):
    levels, count, points = x.shape
    rows = 8 * groups
    kernel = functools.partial(dft_kernel, groups, base, levels, slots)
    flops = 2 * 6 * rows * levels * points * 640
    whole = pl.BlockSpec((32 * rows, 128), lambda g: (0, 0))
    return pl.pallas_call(
        kernel,
        grid=(1,),
        out_shape=(
            jax.ShapeDtypeStruct((32 * rows, 128), jnp.bfloat16),
            jax.ShapeDtypeStruct((32 * rows, 128), jnp.float32),
        ),
        in_specs=[
            pl.BlockSpec(memory_space=pltpu.SMEM),
            pl.BlockSpec(memory_space=pltpu.SMEM),
            pl.BlockSpec((slots // 2, 128), lambda g: (0, 0)),
            pl.BlockSpec(memory_space=pltpu.HBM),
        ],
        out_specs=(whole, whole),
        scratch_shapes=[
            pltpu.VMEM((points // 128 * 64, 128), jnp.float32),
            pltpu.VMEM((points // 128 * 64, 128), jnp.float32),
            pltpu.VMEM((points // 128 * 64, 128), jnp.float32),
            pltpu.VMEM((points // 128 * 64, 128), jnp.float32),
            pltpu.VMEM((256, 256), jnp.bfloat16),
            pltpu.VMEM((8, 128), jnp.float32),
            pltpu.VMEM((16, 128), jnp.float32),
            pltpu.VMEM((4, 128, 128), jnp.float32),
            pltpu.VMEM((64 * rows, 128), jnp.float32),
            pltpu.VMEM((2, levels, 8, points), jnp.float32),
            pltpu.SemaphoreType.DMA((2,)),
        ],
        compiler_params=pltpu.CompilerParams(vmem_limit_bytes=LIMITS[base > 0] * MIB),
        cost_estimate=pl.CostEstimate(flops=flops, bytes_accessed=rows * levels * points * 4, transcendentals=0),
    )(lengths, south, waves, x)


def fold_kernel(chunks, south_ref, *refs):
    n = len(chunks)
    o_ref = refs[-1]
    sign = 1.0 - 2.0 * south_ref[0].astype(jnp.float32)

    def two_owners(j, _):
        parts = [[], [], [], []]
        for i, (_, groups) in enumerate(chunks):
            rows = 16 * groups
            at = pl.ds(pl.multiple_of(j * rows, rows), rows)
            other = refs[i][at, :].astype(jnp.float32)
            mine = refs[n + i][at, :]
            plus = mine + other
            minus = (mine - other) * sign
            for k in range(2):
                parts[2 * k].append(plus[k * rows // 2 : (k + 1) * rows // 2])
                parts[2 * k + 1].append(minus[k * rows // 2 : (k + 1) * rows // 2])
        block = jnp.concatenate([e for part in parts for e in part], axis=0)
        size = block.shape[0]
        o_ref[pl.ds(pl.multiple_of(j * size, size), size), :] = block.astype(jnp.bfloat16)
        return 0

    lax.fori_loop(0, 16, two_owners, 0, unroll=16)


def folded(others, mine, south, chunks):
    total = sum(8 * groups for _, groups in chunks)
    vmem = pl.BlockSpec(memory_space=pltpu.VMEM)
    return pl.pallas_call(
        functools.partial(fold_kernel, chunks),
        out_shape=jax.ShapeDtypeStruct((64 * total, 128), jnp.bfloat16),
        in_specs=[pl.BlockSpec(memory_space=pltpu.SMEM)] + [vmem] * (2 * len(chunks)),
        out_specs=vmem,
        compiler_params=pltpu.CompilerParams(vmem_limit_bytes=16 * MIB),
        cost_estimate=pl.CostEstimate(flops=64 * total * 256, bytes_accessed=0, transcendentals=0),
    )(south, *others, *mine)


def load_kernel(hbm, after, vmem, sem):
    copy = pltpu.make_async_copy(hbm, vmem, sem)
    copy.start()
    copy.wait()


def load(array, after):
    return pl.pallas_call(
        load_kernel,
        out_shape=jax.ShapeDtypeStruct(array.shape, array.dtype),
        in_specs=[pl.BlockSpec(memory_space=pltpu.HBM), pl.BlockSpec(memory_space=pl.ANY)],
        out_specs=pl.BlockSpec(memory_space=pltpu.VMEM),
        scratch_shapes=[pltpu.SemaphoreType.DMA],
        compiler_params=pltpu.CompilerParams(vmem_limit_bytes=16 * MIB),
        cost_estimate=pl.CostEstimate(flops=0, bytes_accessed=array.size * 2, transcendentals=0),
    )(array, after)


def legendre_kernel(levels, slots, half_ref, place_ref, *refs):
    fields = len(refs) - 4
    parts = refs[:fields]
    leg_ref, kept_ref, given_ref, xt = refs[fields:]
    total = parts[0].shape[0]
    width = 2 * levels * slots
    for i, part in enumerate(parts):
        at = pl.multiple_of(place_ref[i] * width, 8)
        for k in range(0, total, 128):
            xt[k // 128, pl.ds(at, width), :] = part[pl.ds(k, 128), :].astype(jnp.float32).T[:width]
    here = half_ref[0] == 0
    tall = fields * 2 * levels

    for s in range(slots):
        lhs = jnp.concatenate([xt[k, pl.ds(s, tall, stride=slots), :] for k in range(total // 128)], axis=1)
        res = jnp.dot(lhs.astype(jnp.bfloat16), leg_ref[s], preferred_element_type=jnp.float32)
        upper, lower = res[: tall // 2], res[tall // 2 :]
        kept_ref[s] = jnp.where(here, upper, lower)
        given_ref[s] = jnp.where(here, lower, upper).astype(given_ref.dtype)


def project(parts, legendre, half, places, levels, slots):
    _, total, coeffs = legendre.shape
    fields = len(parts)
    width = 2 * levels * slots
    tall = fields * 2 * levels
    vmem = pl.BlockSpec(memory_space=pltpu.VMEM)
    smem = pl.BlockSpec(memory_space=pltpu.SMEM)
    return pl.pallas_call(
        functools.partial(legendre_kernel, levels, slots),
        out_shape=(
            jax.ShapeDtypeStruct((slots, tall // 2, coeffs), jnp.float32),
            jax.ShapeDtypeStruct((slots, tall // 2, coeffs), PARTIAL),
        ),
        in_specs=[smem, smem] + [vmem] * (fields + 1),
        out_specs=(vmem, vmem),
        scratch_shapes=[pltpu.VMEM((total // 128, fields * width, 128), jnp.float32)],
        compiler_params=pltpu.CompilerParams(vmem_limit_bytes=24 * MIB),
        cost_estimate=pl.CostEstimate(flops=4 * slots * tall * total * coeffs, bytes_accessed=slots * total * coeffs * 2, transcendentals=0),
    )(half, places, *parts, legendre)


CHUNKS = ((0, 3), (3, 2))
PARTIAL = jnp.bfloat16
LIMITS = (60, 20)
LAG = 1
SPLIT_AT = 4


def body(grid_fields, row_points, wave_order, legendre, helmholtz_tau):
    lat_count = lax.axis_size("lat")
    fld_count = lax.axis_size("fld")
    lat_index = lax.axis_index("lat")
    fld_index = lax.axis_index("fld")
    count, levels, _ = grid_fields.shape
    slots, total, coeffs = legendre.shape
    owners = lat_count // 2
    x = jnp.transpose(grid_fields, (1, 0, 2))
    waves = wave_order.reshape((slots // 2, 128))
    south = (lat_index // owners).astype(jnp.int32).reshape((1,))
    across = [(i, i ^ owners) for i in range(lat_count)]
    sides = [list(range(owners)), list(range(owners, 2 * owners))]
    others, mine = [], []
    for base, groups in CHUNKS:
        give, keep = transform(x, row_points, south, waves, slots, base, groups)
        others.append(lax.ppermute(give, "lat", across))
        mine.append(keep)
    outgoing = folded(others, mine, south, CHUNKS)
    arrived = lax.all_to_all(outgoing, "lat", split_axis=0, concat_axis=0, tiled=True, axis_index_groups=sides)
    legendre = load(legendre, outgoing)
    arrived = arrived.reshape((2, owners // 2, 2, count, 128)).transpose((2, 0, 1, 3, 4)).reshape((fld_count, total, 128))
    parts, places = [], []
    for k in (0, 2, 1, 3):
        block = lax.dynamic_index_in_dim(arrived, fld_index ^ k, 0, keepdims=False)
        if k:
            block = lax.ppermute(block, "fld", [(i, i ^ k) for i in range(fld_count)])
        parts.append(block)
        places.append(fld_index ^ k)
    places = jnp.stack(places).astype(jnp.int32)
    parity = fld_index // 2
    half = fld_index % 2
    kept, given = project(parts, legendre, half.astype(jnp.int32).reshape((1,)), places, levels, slots)
    combined = kept + lax.ppermute(given, "fld", [(i, i ^ 1) for i in range(fld_count)]).astype(jnp.float32)
    half_levels = levels * fld_count // 2
    owned = lax.dynamic_slice_in_dim(wave_order, lat_index * slots, slots)
    degree = owned[:, None] + 2 * jnp.arange(coeffs, dtype=jnp.int32)[None, :] + parity
    degree = degree.astype(jnp.float32)
    shape_term = degree * (degree + 1.0) / float((2 * coeffs) ** 2)
    rates = lax.dynamic_slice_in_dim(helmholtz_tau, half * half_levels, half_levels)
    operator = 1.0 + rates[None, :, None, None] * shape_term[:, None, None, :]
    return combined.reshape((slots, half_levels, 2, coeffs)) / operator


def solution(mesh):
    in_specs = (P("lat", "fld", None), P("lat"), P(), P("lat", "fld", None), P())
    out_specs = P("lat", "fld", None, None)
    return jax.shard_map(body, mesh=mesh, in_specs=in_specs, out_specs=out_specs, check_vma=False)
```
